32 devices in a mesh: groups: 2 (over x), lon: 16 (over z, y, core).
Axes of the slice: x: 2, y: 2, z: 4, core: 2. Of those that a mesh axis runs over, the one named last changes fastest.
Arguments:
- source: bfloat16 [32, 1024, 256], P('groups', 'lon'), parts along dimension 0, may hold values from -6 to 6
- quadrature: bfloat16 [9, 16, 6, 64], replicated, may hold values from -0.29882812 to 0.29882812
- block_rows: int32 [16, 6], replicated, may hold values from 0 to 15, as said below
- offsets: int32 [16, 6], replicated, may hold values from -64 to 0
- counts: int32 [16], replicated, may hold values from 1 to 6, as said below
- weight: bfloat16 [9, 256, 256], replicated, may hold values from -0.125 to 0.125
- cotangent: bfloat16 [32, 1024, 256], P('groups', 'lon'), parts along dimension 0, may hold values from -6 to 6
Outputs:
- mixed: bfloat16 [32, 1024, 256], P('groups', 'lon'), parts along dimension 0
- grad_source: float32 [32, 1024, 256], P('groups', 'lon'), parts along dimension 0
- grad_weight: float32 [18, 256, 256], P('groups'), parts along dimension 0
The draws below stay inside these ranges and needn't reach their ends.
There are 2 independent parts, one for each index of `groups`. The reference program is written for one: setup_inputs(seed, part) draws one part's arguments, and reference() takes and returns one part's arrays. A program takes and returns all parts, laid end to end along the dimension named above; an argument that names none is the same for every part. Nothing has to cross between parts.
Inputs may be any that keep to these rules, and one draw needn't show every extreme that they name: `block_rows`: within 3 rows of the output row. `counts`: blocks at or past the count are ignored.
All inputs are finite; a program needn't handle non-finite values.
Results may differ from the reference program's by a relative error of at most 0.0049.
Values may be sent and summed in bfloat16 or wider, within the bound.
A program may use at most 128 MiB of HBM per device.

```python
import math
import jax
import jax.numpy as jnp
from jax import lax

CH = 256
K = 9
PW = 64
NB = 6
LAT = 16
NLON = 1024


def draw_block_rows(key, part):
    key = jax.random.fold_in(key, 11)
    jitter = jax.random.randint(key, (LAT, NB), -3, 4)
    picked = jnp.clip(jnp.arange(LAT, dtype=jnp.int32)[:, None] + jitter, 0, LAT - 1)
    picked = picked.at[0, 0].set(0).at[LAT - 1, 0].set(LAT - 1)
    return picked.astype(jnp.int32)


def draw_offsets(key, part):
    key = jax.random.fold_in(key, 23)
    picked = jax.random.randint(key, (LAT, NB), -PW, 1)
    picked = picked.at[0, 0].set(-PW).at[0, 1].set(0)
    return picked.astype(jnp.int32)


def draw_counts(key, part):
    key = jax.random.fold_in(key, 37)
    picked = jax.random.randint(key, (LAT,), 1, NB + 1)
    picked = picked.at[0].set(NB).at[LAT - 1].set(1)
    return picked.astype(jnp.int32)


def level_of(rng, shape, cuts, smallest, top_value):
    def one(axis_at, parts):
        heights = jax.random.uniform(jax.random.fold_in(jax.random.fold_in(rng, 6), axis_at), (parts,), jnp.float32, smallest / len(cuts), top_value / len(cuts))
        return jnp.repeat(jnp.exp(heights), shape[axis_at] // parts).reshape((-1,) + (1,) * (len(shape) - axis_at - 1))

    factor_of = one(*cuts[0])
    for cut in cuts[1:]:
        factor_of = factor_of * one(*cut)
    return factor_of


def scatter_about(stream_key, extent, width, limit, shards=(), kind=jnp.bfloat16):
    result = jax.random.normal(stream_key, extent, jnp.float32) * width
    if len(shards) > 0:
        result = level_of(stream_key, extent, shards, -0.22, 0.18) * result
    return jnp.clip(result, min=-limit, max=limit).astype(kind)


def setup_inputs(seed: int = 0, part: int = 0) -> dict:
    key_list = jax.random.split(jax.random.key(seed), 8)
    part_splits = jax.random.split(jax.random.fold_in(key_list[7], part), 8)
    source = scatter_about(part_splits[0], (LAT, NLON, CH), 1.0, 6.0, ((1, 16),))
    quadrature = scatter_about(key_list[1], (K, LAT, NB, PW), 0.05, 0.29882812)
    block_rows = draw_block_rows(jax.random.fold_in(key_list[7], 71), part)
    offsets = draw_offsets(jax.random.fold_in(key_list[7], 71), part)
    counts = draw_counts(jax.random.fold_in(key_list[7], 71), part)
    weight = scatter_about(key_list[5], (K, CH, CH), (K * CH) ** -0.5, 0.125)
    cotangent = scatter_about(part_splits[6], (LAT, NLON, CH), 1.0, 6.0, ((1, 16),))
    return {"source": source, "quadrature": quadrature, "block_rows": block_rows, "offsets": offsets, "counts": counts, "weight": weight, "cotangent": cotangent}


def reference(source, quadrature, block_rows, offsets, counts, weight, cotangent):
    lat_rows, lon_total, channels = source.shape
    filters = weight.shape[0]
    blocks = block_rows.shape[1]
    stencil = quadrature.shape[3]
    alive = (jnp.arange(blocks, dtype=jnp.int32)[None, :] < counts[:, None]).astype(jnp.float32)
    taps = jnp.transpose(quadrature.astype(jnp.float32), (1, 2, 0, 3)) * alive[:, :, None, None]
    longitude = jnp.arange(lon_total, dtype=jnp.int32)
    tap_ids = jnp.arange(stencil, dtype=jnp.int32)

    def columns(offset_one):
        return ((longitude[:, None] + offset_one + tap_ids[None, :]) % lon_total).astype(jnp.int32)

    def conv_row(i):
        total = jnp.zeros((lon_total, filters, channels), jnp.float32)
        for b in range(blocks):
            source_row = jnp.take(source, block_rows[i, b], axis=0)
            windowed = jnp.take(source_row, columns(offsets[i, b]), axis=0).astype(jnp.float32)
            total = total + jnp.einsum('jtc,kt->jkc', windowed, taps[i, b])
        return total.astype(jnp.bfloat16)
    basis = lax.map(conv_row, jnp.arange(lat_rows, dtype=jnp.int32))
    flat_basis = basis.reshape(lat_rows * lon_total, filters * channels)
    mix_matrix = weight.reshape(filters * channels, channels)
    mixed = jnp.dot(flat_basis, mix_matrix, preferred_element_type=jnp.float32).astype(jnp.bfloat16)
    mixed = mixed.reshape(lat_rows, lon_total, channels)
    flat_grad = cotangent.reshape(lat_rows * lon_total, channels)
    grad_basis = lax.dot_general(flat_grad, mix_matrix, (((1,), (1,)), ((), ())), preferred_element_type=jnp.float32).astype(jnp.bfloat16)
    grad_basis = grad_basis.reshape(lat_rows, lon_total, filters, channels)

    def spread(i, total):
        grad_row = jnp.take(grad_basis, i, axis=0).astype(jnp.float32)
        for b in range(blocks):
            pieces = jnp.einsum('jkc,kt->jtc', grad_row, taps[i, b])
            total = total.at[block_rows[i, b], columns(offsets[i, b])].add(pieces)
        return total
    grad_source = lax.fori_loop(0, lat_rows, spread, jnp.zeros((lat_rows, lon_total, channels), jnp.float32))
    factor = 1.0 / math.sqrt(lat_rows * lon_total)
    local_grad = lax.dot_general(flat_basis, flat_grad, (((0,), (0,)), ((), ())), preferred_element_type=jnp.float32)
    grad_weight = (local_grad * factor).reshape(filters, channels, channels)
    return (mixed, grad_source, grad_weight)
```

```python
import math

import jax
import jax.numpy as jnp
from jax import lax
from jax.experimental import pallas as pl
from jax.experimental.pallas import tpu as pltpu
from jax.sharding import PartitionSpec as P

VM = pl.BlockSpec(memory_space=pltpu.VMEM)
SM = pl.BlockSpec(memory_space=pltpu.SMEM)


def build_band(i, counts, quad, band, filters, blocks, cols):
    for b in range(blocks):
        live = (b < counts[i]).astype(jnp.float32)
        for k in range(filters):
            row = quad[k, i, pl.ds(b, 1), :] * live
            wide = jnp.broadcast_to(row, (cols, row.shape[1]))
            wide = pltpu.roll(wide, 0, 1, stride=1, stride_axis=0)
            band[k * cols : (k + 1) * cols, b * 128 : (b + 1) * 128] = wide.astype(jnp.bfloat16)


def forward_kernel(counts, rows, offs, before, source, after, quad, weight, cot, mixed, grad, ext, band, picked, basis):
    lat, cols, ch = source.shape
    filters = quad.shape[0]
    blocks = rows.shape[1]
    reach = before.shape[1]
    ext[:, :reach, :] = before[...].astype(jnp.float32)
    ext[:, reach : reach + cols, :] = source[...].astype(jnp.float32)
    ext[:, reach + cols : 2 * reach + cols, :] = after[...].astype(jnp.float32)

    def step(i, _):
        build_band(i, counts, quad, band, filters, blocks, cols)
        for b in range(blocks):
            start = offs[i, b] + reach
            shift = start % 8
            near = ext[rows[i, b], pl.ds(pl.multiple_of(start - shift, 8), 136), :].reshape(17, 8, ch)
            near = pltpu.roll(near, (8 - shift) % 8, 1)
            place = lax.broadcasted_iota(jnp.int32, (16, 8, ch), 1)
            near = jnp.where(place < 8 - shift, near[:16], near[1:]).reshape(128, ch)
            picked[b * 128 : (b + 1) * 128, :] = near.astype(jnp.bfloat16)
        here = pl.ds(pl.multiple_of(i * cols, cols), cols)
        out = jnp.dot(band[...], picked[...], preferred_element_type=jnp.float32).astype(jnp.bfloat16)
        for k in range(filters):
            basis[here, k * ch : (k + 1) * ch] = out[k * cols : (k + 1) * cols]
        return 0

    lax.fori_loop(0, lat, step, 0)
    total = lat * cols
    tile = 256

    def mix(m, _):
        here = pl.ds(pl.multiple_of(m * tile, tile), tile)
        mixed[here, :] = jnp.dot(basis[here, :], weight[...], preferred_element_type=jnp.float32).astype(jnp.bfloat16)
        return 0

    lax.fori_loop(0, total // tile, mix, 0)
    for k in range(filters):
        here = slice(k * ch, (k + 1) * ch)
        grad[here, :] = lax.dot_general(
            basis[:, here], cot[...], (((0,), (0,)), ((), ())), preferred_element_type=jnp.float32
        )


def backward_kernel(counts, rows, offs, quad, weight, cot, inner, west, east, total, band, grads):
    lat, cols, ch = inner.shape
    filters = quad.shape[0]
    blocks = rows.shape[1]
    reach = west.shape[1]
    total[...] = jnp.zeros_like(total)
    for k in range(filters):
        part = lax.dot_general(
            cot[...],
            weight[k * ch : (k + 1) * ch, :],
            (((1,), (1,)), ((), ())),
            preferred_element_type=jnp.float32,
        ).astype(jnp.bfloat16)
        grads[:, k * cols : (k + 1) * cols, :] = part.reshape(lat, cols, ch)

    def step(i, _):
        build_band(i, counts, quad, band, filters, blocks, cols)
        parts = lax.dot_general(
            band[...], grads[i], (((0,), (0,)), ((), ())), preferred_element_type=jnp.float32
        )
        for b in range(blocks):
            start = offs[i, b] + reach
            shift = start % 8
            far = pltpu.roll(parts[b * 128 : (b + 1) * 128].reshape(16, 8, ch), shift, 1)
            zero = jnp.zeros((1, 8, ch), jnp.float32)
            place = lax.broadcasted_iota(jnp.int32, (17, 8, ch), 1)
            far = jnp.where(
                place >= shift, jnp.concatenate([far, zero], axis=0), jnp.concatenate([zero, far], axis=0)
            )
            here = pl.ds(pl.multiple_of(start - shift, 8), 136)
            total[rows[i, b], here, :] += far.reshape(136, ch)
        return 0

    lax.fori_loop(0, lat, step, 0)
    west[...] = total[:, :reach, :].astype(jnp.bfloat16)
    inner[...] = total[:, reach : reach + cols, :]
    east[...] = total[:, reach + cols : 2 * reach + cols, :].astype(jnp.bfloat16)


def shards(source, quadrature, block_rows, offsets, counts, weight, cotangent):
    lat, cols, ch = source.shape
    filters = weight.shape[0]
    blocks = block_rows.shape[1]
    reach = quadrature.shape[3]
    peers = lax.axis_size("lon")
    up = [(i, (i + 1) % peers) for i in range(peers)]
    down = [(j, i) for i, j in up]
    before = lax.ppermute(source[:, cols - reach :], "lon", up)
    after = lax.ppermute(source[:, :reach], "lon", down)
    quad = jnp.pad(quadrature.astype(jnp.float32), ((0, 0), (0, 0), (0, 0), (0, 128 - reach)))
    flat_weight = weight.reshape(filters * ch, ch)
    flat_cot = cotangent.reshape(lat * cols, ch)
    params = pltpu.CompilerParams(vmem_limit_bytes=48 * 2**20)
    wide = cols + 2 * reach + 8
    mixed, local = pl.pallas_call(
        forward_kernel,
        out_shape=[
            jax.ShapeDtypeStruct((lat * cols, ch), jnp.bfloat16),
            jax.ShapeDtypeStruct((filters * ch, ch), jnp.float32),
        ],
        in_specs=[SM] * 3 + [VM] * 6,
        out_specs=[VM] * 2,
        scratch_shapes=[
            pltpu.VMEM((lat, wide, ch), jnp.float32),
            pltpu.VMEM((filters * cols, blocks * 128), jnp.bfloat16),
            pltpu.VMEM((blocks * 128, ch), jnp.bfloat16),
            pltpu.VMEM((lat * cols, filters * ch), jnp.bfloat16),
        ],
        compiler_params=params,
        cost_estimate=pl.CostEstimate(flops=8_000_000_000, bytes_accessed=8_000_000, transcendentals=0),
        name="forward",
    )(counts, block_rows, offsets, before, source, after, quad, flat_weight, flat_cot)
    inner, west, east = pl.pallas_call(
        backward_kernel,
        out_shape=[
            jax.ShapeDtypeStruct((lat, cols, ch), jnp.float32),
            jax.ShapeDtypeStruct((lat, reach, ch), jnp.bfloat16),
            jax.ShapeDtypeStruct((lat, reach, ch), jnp.bfloat16),
        ],
        in_specs=[SM] * 3 + [VM] * 3,
        out_specs=[VM] * 3,
        scratch_shapes=[
            pltpu.VMEM((lat, wide, ch), jnp.float32),
            pltpu.VMEM((filters * cols, blocks * 128), jnp.bfloat16),
            pltpu.VMEM((lat, filters * cols, ch), jnp.bfloat16),
        ],
        compiler_params=params,
        cost_estimate=pl.CostEstimate(flops=8_000_000_000, bytes_accessed=8_000_000, transcendentals=0),
        name="backward",
    )(counts, block_rows, offsets, quad, flat_weight, flat_cot)
    summed = lax.psum(local, "lon")
    factor = 1.0 / math.sqrt(lat * cols * peers)
    grad_weight = (summed * factor).reshape(filters, ch, ch)
    west_in = lax.ppermute(east, "lon", up).astype(jnp.float32)
    east_in = lax.ppermute(west, "lon", down).astype(jnp.float32)
    inner = inner.at[:, :reach].add(west_in)
    grad_source = inner.at[:, cols - reach :].add(east_in)
    return (mixed.reshape(lat, cols, ch), grad_source, grad_weight)


def solution(mesh):
    return jax.shard_map(
        shards,
        mesh=mesh,
        in_specs=(P("groups", "lon", None), P(), P(), P(), P(), P(), P("groups", "lon", None)),
        out_specs=(P("groups", "lon", None), P("groups", "lon", None), P("groups", None, None)),
        check_vma=False,
    )
```

```python
import math

import jax
import jax.numpy as jnp
from jax import lax
from jax.experimental import pallas as pl
from jax.experimental.pallas import tpu as pltpu
from jax.sharding import PartitionSpec as P

VM = pl.BlockSpec(memory_space=pltpu.VMEM)
MESH = pl.DeviceIdType.MESH
SM = pl.BlockSpec(memory_space=pltpu.SMEM)


def build_band(i, counts, quad, band, filters, blocks, cols):
    for b in range(blocks):
        live = (b < counts[i]).astype(jnp.float32)
        for k in range(filters):
            row = quad[k, i, pl.ds(b, 1), :] * live
            wide = jnp.broadcast_to(row, (cols, row.shape[1]))
            wide = pltpu.roll(wide, 0, 1, stride=1, stride_axis=0)
            band[k * cols : (k + 1) * cols, b * 128 : (b + 1) * 128] = wide.astype(jnp.bfloat16)


def forward_kernel(counts, rows, offs, before, source, after, quad, weight, cot, mixed, grad, ext, band, picked, basis):
    lat, cols, ch = source.shape
    filters = quad.shape[0]
    blocks = rows.shape[1]
    reach = before.shape[1]
    ext[:, :reach, :] = before[...].astype(jnp.float32)
    ext[:, reach : reach + cols, :] = source[...].astype(jnp.float32)
    ext[:, reach + cols : 2 * reach + cols, :] = after[...].astype(jnp.float32)

    def step(i, _):
        build_band(i, counts, quad, band, filters, blocks, cols)
        for b in range(blocks):
            start = offs[i, b] + reach
            shift = start % 8
            near = ext[rows[i, b], pl.ds(pl.multiple_of(start - shift, 8), 136), :].reshape(17, 8, ch)
            near = pltpu.roll(near, (8 - shift) % 8, 1)
            place = lax.broadcasted_iota(jnp.int32, (16, 8, ch), 1)
            near = jnp.where(place < 8 - shift, near[:16], near[1:]).reshape(128, ch)
            picked[b * 128 : (b + 1) * 128, :] = near.astype(jnp.bfloat16)
        here = pl.ds(pl.multiple_of(i * cols, cols), cols)
        out = jnp.dot(band[...], picked[...], preferred_element_type=jnp.float32).astype(jnp.bfloat16)
        for k in range(filters):
            basis[here, k * ch : (k + 1) * ch] = out[k * cols : (k + 1) * cols]
        return 0

    lax.fori_loop(0, lat, step, 0)
    total = lat * cols
    tile = 256

    def mix(m, _):
        here = pl.ds(pl.multiple_of(m * tile, tile), tile)
        mixed[here, :] = jnp.dot(basis[here, :], weight[...], preferred_element_type=jnp.float32).astype(jnp.bfloat16)
        return 0

    lax.fori_loop(0, total // tile, mix, 0)
    for k in range(filters):
        here = slice(k * ch, (k + 1) * ch)
        grad[here, :] = lax.dot_general(
            basis[:, here], cot[...], (((0,), (0,)), ((), ())), preferred_element_type=jnp.float32
        ).astype(jnp.bfloat16)
    if grad.shape[0] > filters * ch:
        grad[filters * ch :, :] = jnp.zeros((grad.shape[0] - filters * ch, ch), jnp.bfloat16)


def backward_kernel(counts, rows, offs, quad, weight, cot, inner, west, east, total, band, grads):
    lat, cols, ch = inner.shape
    filters = quad.shape[0]
    blocks = rows.shape[1]
    reach = west.shape[1]
    total[...] = jnp.zeros_like(total)
    for k in range(filters):
        part = lax.dot_general(
            cot[...],
            weight[k * ch : (k + 1) * ch, :],
            (((1,), (1,)), ((), ())),
            preferred_element_type=jnp.float32,
        ).astype(jnp.bfloat16)
        grads[:, k * cols : (k + 1) * cols, :] = part.reshape(lat, cols, ch)

    def step(i, _):
        build_band(i, counts, quad, band, filters, blocks, cols)
        parts = lax.dot_general(
            band[...], grads[i], (((0,), (0,)), ((), ())), preferred_element_type=jnp.float32
        )
        for b in range(blocks):
            start = offs[i, b] + reach
            shift = start % 8
            far = pltpu.roll(parts[b * 128 : (b + 1) * 128].reshape(16, 8, ch), shift, 1)
            zero = jnp.zeros((1, 8, ch), jnp.float32)
            place = lax.broadcasted_iota(jnp.int32, (17, 8, ch), 1)
            far = jnp.where(
                place >= shift, jnp.concatenate([far, zero], axis=0), jnp.concatenate([zero, far], axis=0)
            )
            here = pl.ds(pl.multiple_of(start - shift, 8), 136)
            total[rows[i, b], here, :] += far.reshape(136, ch)
        return 0

    lax.fori_loop(0, lat, step, 0)
    west[...] = total[:, :reach, :].astype(jnp.bfloat16)
    inner[...] = total[:, reach : reach + cols, :]
    east[...] = total[:, reach + cols : 2 * reach + cols, :].astype(jnp.bfloat16)


def sum_kernel(mine, out, paired, partial, others, sems):
    groups, rows, ch = partial.shape
    me = lax.axis_index("lon")
    core = lax.rem(me, 2)
    chip = lax.div(me, 2)
    sibling = chip * 2 + 1 - core
    peer = [lax.rem(chip + d, groups) * 2 + core for d in range(groups)]
    barrier = pltpu.get_barrier_semaphore()
    for other in [sibling] + peer[1:]:
        pl.semaphore_signal(barrier, inc=1, device_id={"lon": other}, device_id_type=MESH)
    pl.semaphore_wait(barrier, groups)

    def copy(src, dst, phase, slot, other):
        return pltpu.make_async_remote_copy(
            src_ref=src,
            dst_ref=dst,
            send_sem=sems.at[phase, 0, slot],
            recv_sem=sems.at[phase, 1, slot],
            device_id={"lon": other},
            device_id_type=MESH,
        )

    pairs = []
    for d in list(range(1, groups)) + [0]:
        q = lax.rem(chip + d, groups)
        pairs.append((d, q, copy(mine.at[1 - core, q], paired.at[d], 0, d, sibling)))
        pairs[-1][2].start()
    crossing = []
    for d, q, pair in pairs:
        pair.wait()
        both = mine[core, q].astype(jnp.float32) + paired[d].astype(jnp.float32)
        partial[d] = both.astype(jnp.bfloat16)
        if d > 0:
            crossing.append(copy(partial.at[d], others.at[d], 1, d, peer[d]))
            crossing[-1].start()
    total = partial[0].astype(jnp.float32)
    for d in range(1, groups):
        crossing[d - 1].wait()
        total = total + others[d].astype(jnp.float32)
    out[core, chip] = total.astype(jnp.bfloat16)
    spread = []
    for d in range(1, groups):
        spread.append(copy(out.at[core, chip], out.at[core, chip], 2, d, peer[d]))
        spread[-1].start()
    handed = [copy(out.at[core, chip], out.at[core, chip], 3, 0, sibling)]
    handed[0].start()
    for d in range(1, groups):
        spread[d - 1].wait()
        came = lax.rem(chip - d + groups, groups)
        handed.append(copy(out.at[core, came], out.at[core, came], 3, d, sibling))
        handed[-1].start()
    for one in handed:
        one.wait()


def shards(source, quadrature, block_rows, offsets, counts, weight, cotangent):
    lat, cols, ch = source.shape
    filters = weight.shape[0]
    blocks = block_rows.shape[1]
    reach = quadrature.shape[3]
    peers = lax.axis_size("lon")
    up = [(i, (i + 1) % peers) for i in range(peers)]
    down = [(j, i) for i, j in up]
    before = lax.ppermute(source[:, cols - reach :], "lon", up)
    after = lax.ppermute(source[:, :reach], "lon", down)
    quad = jnp.pad(quadrature.astype(jnp.float32), ((0, 0), (0, 0), (0, 0), (0, 128 - reach)))
    flat_weight = weight.reshape(filters * ch, ch)
    flat_cot = cotangent.reshape(lat * cols, ch)
    params = pltpu.CompilerParams(vmem_limit_bytes=48 * 2**20)
    chunk = -(-filters * ch // (16 * peers)) * 16
    wide = cols + 2 * reach + 8
    mixed, local = pl.pallas_call(
        forward_kernel,
        out_shape=[
            jax.ShapeDtypeStruct((lat * cols, ch), jnp.bfloat16),
            jax.ShapeDtypeStruct((peers * chunk, ch), jnp.bfloat16),
        ],
        in_specs=[SM] * 3 + [VM] * 6,
        out_specs=[VM] * 2,
        scratch_shapes=[
            pltpu.VMEM((lat, wide, ch), jnp.float32),
            pltpu.VMEM((filters * cols, blocks * 128), jnp.bfloat16),
            pltpu.VMEM((blocks * 128, ch), jnp.bfloat16),
            pltpu.VMEM((lat * cols, filters * ch), jnp.bfloat16),
        ],
        compiler_params=params,
        cost_estimate=pl.CostEstimate(flops=8_000_000_000, bytes_accessed=8_000_000, transcendentals=0),
        name="forward",
    )(counts, block_rows, offsets, before, source, after, quad, flat_weight, flat_cot)
    inner, west, east = pl.pallas_call(
        backward_kernel,
        out_shape=[
            jax.ShapeDtypeStruct((lat, cols, ch), jnp.float32),
            jax.ShapeDtypeStruct((lat, reach, ch), jnp.bfloat16),
            jax.ShapeDtypeStruct((lat, reach, ch), jnp.bfloat16),
        ],
        in_specs=[SM] * 3 + [VM] * 3,
        out_specs=[VM] * 3,
        scratch_shapes=[
            pltpu.VMEM((lat, wide, ch), jnp.float32),
            pltpu.VMEM((filters * cols, blocks * 128), jnp.bfloat16),
            pltpu.VMEM((lat, filters * cols, ch), jnp.bfloat16),
        ],
        compiler_params=params,
        cost_estimate=pl.CostEstimate(flops=8_000_000_000, bytes_accessed=8_000_000, transcendentals=0),
        name="backward",
    )(counts, block_rows, offsets, quad, flat_weight, flat_cot)
    groups = peers // 2
    summed = pl.pallas_call(
        sum_kernel,
        out_shape=jax.ShapeDtypeStruct((2, groups, chunk, ch), jnp.bfloat16),
        in_specs=[VM],
        out_specs=VM,
        scratch_shapes=[pltpu.VMEM((groups, chunk, ch), jnp.bfloat16)] * 3
        + [pltpu.SemaphoreType.DMA((4, 2, groups))],
        compiler_params=pltpu.CompilerParams(
            vmem_limit_bytes=32 * 2**20, collective_id=0, has_side_effects=True
        ),
        cost_estimate=pl.CostEstimate(flops=30_000_000_000, bytes_accessed=60_000_000, transcendentals=0),
        name="weight_sum",
    )(local.reshape(2, groups, chunk, ch))
    summed = summed.reshape(peers * chunk, ch)[: filters * ch].astype(jnp.float32)
    factor = 1.0 / math.sqrt(lat * cols * peers)
    grad_weight = (summed * factor).reshape(filters, ch, ch)
    west_in = lax.ppermute(east, "lon", up).astype(jnp.float32)
    east_in = lax.ppermute(west, "lon", down).astype(jnp.float32)
    inner = inner.at[:, :reach].add(west_in)
    grad_source = inner.at[:, cols - reach :].add(east_in)
    return (mixed.reshape(lat, cols, ch), grad_source, grad_weight)


def solution(mesh):
    return jax.shard_map(
        shards,
        mesh=mesh,
        in_specs=(P("groups", "lon", None), P(), P(), P(), P(), P(), P("groups", "lon", None)),
        out_specs=(P("groups", "lon", None), P("groups", "lon", None), P("groups", None, None)),
        check_vma=False,
    )
```

```python
import math

import jax
import jax.numpy as jnp
from jax import lax
from jax.experimental import pallas as pl
from jax.experimental.pallas import tpu as pltpu
from jax.sharding import PartitionSpec as P

VM = pl.BlockSpec(memory_space=pltpu.VMEM)
MESH = pl.DeviceIdType.MESH
SM = pl.BlockSpec(memory_space=pltpu.SMEM)


def by_count(count, blocks, run):
    for n in range(2, blocks + 1, 2):
        pl.when((count > n - 2) & (count <= n))(lambda n=n: run(n))


def build_band(i, counts, quad, band, filters, blocks, cols):
    for b in range(blocks):
        live = (b < counts[i]).astype(jnp.float32)
        for k in range(filters):
            row = quad[k, i, pl.ds(b, 1), :] * live
            wide = jnp.broadcast_to(row, (cols, row.shape[1]))
            wide = pltpu.roll(wide, 0, 1, stride=1, stride_axis=0)
            band[k * cols : (k + 1) * cols, b * 128 : (b + 1) * 128] = wide.astype(jnp.bfloat16)


def forward_kernel(counts, rows, offs, before, source, after, quad, weight, cot, mixed, grad, ext, band, picked, basis):
    lat, cols, ch = source.shape
    filters = quad.shape[0]
    blocks = rows.shape[1]
    reach = before.shape[1]
    ext[:, :reach, :] = before[...].astype(jnp.float32)
    ext[:, reach : reach + cols, :] = source[...].astype(jnp.float32)
    ext[:, reach + cols : 2 * reach + cols, :] = after[...].astype(jnp.float32)

    def live_step(i, blocks):
        build_band(i, counts, quad, band, filters, blocks, cols)
        for b in range(blocks):
            start = offs[i, b] + reach
            shift = start % 8
            near = ext[rows[i, b], pl.ds(pl.multiple_of(start - shift, 8), 136), :].reshape(17, 8, ch)
            near = pltpu.roll(near, (8 - shift) % 8, 1)
            place = lax.broadcasted_iota(jnp.int32, (16, 8, ch), 1)
            near = jnp.where(place < 8 - shift, near[:16], near[1:]).reshape(128, ch)
            picked[b * 128 : (b + 1) * 128, :] = near.astype(jnp.bfloat16)
        here = pl.ds(pl.multiple_of(i * cols, cols), cols)
        used = slice(0, blocks * 128)
        out = jnp.dot(band[:, used], picked[used, :], preferred_element_type=jnp.float32).astype(jnp.bfloat16)
        for k in range(filters):
            basis[here, k * ch : (k + 1) * ch] = out[k * cols : (k + 1) * cols]

    def step(i, _):
        by_count(counts[i], blocks, lambda n: live_step(i, n))
        return 0

    lax.fori_loop(0, lat, step, 0)
    total = lat * cols
    tile = 256

    def mix(m, _):
        here = pl.ds(pl.multiple_of(m * tile, tile), tile)
        mixed[here, :] = jnp.dot(basis[here, :], weight[...], preferred_element_type=jnp.float32).astype(jnp.bfloat16)
        return 0

    lax.fori_loop(0, total // tile, mix, 0)
    for k in range(filters):
        here = slice(k * ch, (k + 1) * ch)
        grad[here, :] = lax.dot_general(
            basis[:, here], cot[...], (((0,), (0,)), ((), ())), preferred_element_type=jnp.float32
        ).astype(jnp.bfloat16)
    if grad.shape[0] > filters * ch:
        grad[filters * ch :, :] = jnp.zeros((grad.shape[0] - filters * ch, ch), jnp.bfloat16)


def backward_kernel(counts, rows, offs, quad, weight, cot, inner, west, east, total, band, grads):
    lat, cols, ch = inner.shape
    filters = quad.shape[0]
    blocks = rows.shape[1]
    reach = west.shape[1]
    total[...] = jnp.zeros_like(total)
    for k in range(filters):
        part = lax.dot_general(
            cot[...],
            weight[k * ch : (k + 1) * ch, :],
            (((1,), (1,)), ((), ())),
            preferred_element_type=jnp.float32,
        ).astype(jnp.bfloat16)
        grads[:, k * cols : (k + 1) * cols, :] = part.reshape(lat, cols, ch)

    def live_step(i, blocks):
        build_band(i, counts, quad, band, filters, blocks, cols)
        parts = lax.dot_general(
            band[:, : blocks * 128], grads[i], (((0,), (0,)), ((), ())), preferred_element_type=jnp.float32
        )
        for b in range(blocks):
            start = offs[i, b] + reach
            shift = start % 8
            far = pltpu.roll(parts[b * 128 : (b + 1) * 128].reshape(16, 8, ch), shift, 1)
            zero = jnp.zeros((1, 8, ch), jnp.float32)
            place = lax.broadcasted_iota(jnp.int32, (17, 8, ch), 1)
            far = jnp.where(
                place >= shift, jnp.concatenate([far, zero], axis=0), jnp.concatenate([zero, far], axis=0)
            )
            here = pl.ds(pl.multiple_of(start - shift, 8), 136)
            total[rows[i, b], here, :] += far.reshape(136, ch)

    def step(i, _):
        by_count(counts[i], blocks, lambda n: live_step(i, n))
        return 0

    lax.fori_loop(0, lat, step, 0)
    west[...] = total[:, :reach, :].astype(jnp.bfloat16)
    inner[...] = total[:, reach : reach + cols, :]
    east[...] = total[:, reach + cols : 2 * reach + cols, :].astype(jnp.bfloat16)


def sum_kernel(mine, out, paired, half, level, partial, others, sems):
    groups, rows, ch = partial.shape
    me = lax.axis_index("lon")
    core = lax.rem(me, 2)
    side = lax.rem(lax.div(me, 2), 2)
    ring = lax.div(me, 4)
    sibling = me + 1 - 2 * core
    across = me + 2 - 4 * side
    spot = [lax.rem(ring + d, groups) for d in range(groups)]
    peer = [spot[d] * 4 + side * 2 + core for d in range(groups)]
    barrier = pltpu.get_barrier_semaphore()
    for other in [sibling, across] + peer[1:]:
        pl.semaphore_signal(barrier, inc=1, device_id={"lon": other}, device_id_type=MESH)
    pl.semaphore_wait(barrier, groups + 1)

    def send(src, dst, phase, slot, other):
        copy = pltpu.make_async_remote_copy(
            src_ref=src,
            dst_ref=dst,
            send_sem=sems.at[phase, 0, slot],
            recv_sem=sems.at[phase, 1, slot],
            device_id={"lon": other},
            device_id_type=MESH,
        )
        copy.start()
        return copy

    order = list(range(1, groups)) + [0]
    line = [side, 1 - side]
    pairs = {}
    for t in (1, 0):
        for d in order:
            pairs[t, d] = send(mine.at[1 - core, line[t], spot[d]], paired.at[t, d], 0, t * groups + d, sibling)

    def both(t, d):
        pairs[t, d].wait()
        return mine[core, line[t], spot[d]].astype(jnp.float32) + paired[t, d].astype(jnp.float32)

    sides = {}
    for d in order:
        half[d] = both(1, d).astype(jnp.bfloat16)
        sides[d] = send(half.at[d], level.at[d], 1, d, across)
    crossing = {}
    for d in order:
        own = both(0, d)
        sides[d].wait()
        own = own + level[d].astype(jnp.float32)
        if d > 0:
            partial[d] = own.astype(jnp.bfloat16)
            crossing[d] = send(partial.at[d], others.at[d], 2, d, peer[d])
    for d in range(1, groups):
        crossing[d].wait()
        own = own + others[d].astype(jnp.float32)
    out[core, side, ring] = own.astype(jnp.bfloat16)

    def share(c, slot, phase, place, other):
        ref = out.at[core, c, place]
        return send(ref, ref, phase, slot, other)

    far = [share(side, d, 3, ring, peer[d]) for d in range(1, groups)]
    near = []
    last = []
    for d in range(groups):
        if d > 0:
            far[d - 1].wait()
        came = lax.rem(ring - d + groups, groups)
        near.append(share(side, d, 4, came, across))
        last.append(share(side, d, 5, came, sibling))
    for d in range(groups):
        near[d].wait()
        came = lax.rem(ring - d + groups, groups)
        last.append(share(1 - side, groups + d, 5, came, sibling))
    for one in last:
        one.wait()


def shards(source, quadrature, block_rows, offsets, counts, weight, cotangent):
    lat, cols, ch = source.shape
    filters = weight.shape[0]
    blocks = block_rows.shape[1]
    reach = quadrature.shape[3]
    peers = lax.axis_size("lon")
    up = [(i, (i + 1) % peers) for i in range(peers)]
    down = [(j, i) for i, j in up]
    before = lax.ppermute(source[:, cols - reach :], "lon", up)
    after = lax.ppermute(source[:, :reach], "lon", down)
    quad = jnp.pad(quadrature.astype(jnp.float32), ((0, 0), (0, 0), (0, 0), (0, 128 - reach)))
    flat_weight = weight.reshape(filters * ch, ch)
    flat_cot = cotangent.reshape(lat * cols, ch)
    params = pltpu.CompilerParams(vmem_limit_bytes=48 * 2**20)
    chunk = -(-filters * ch // (16 * peers)) * 16
    wide = cols + 2 * reach + 8
    mixed, local = pl.pallas_call(
        forward_kernel,
        out_shape=[
            jax.ShapeDtypeStruct((lat * cols, ch), jnp.bfloat16),
            jax.ShapeDtypeStruct((peers * chunk, ch), jnp.bfloat16),
        ],
        in_specs=[SM] * 3 + [VM] * 6,
        out_specs=[VM] * 2,
        scratch_shapes=[
            pltpu.VMEM((lat, wide, ch), jnp.float32),
            pltpu.VMEM((filters * cols, blocks * 128), jnp.bfloat16),
            pltpu.VMEM((blocks * 128, ch), jnp.bfloat16),
            pltpu.VMEM((lat * cols, filters * ch), jnp.bfloat16),
        ],
        compiler_params=params,
        cost_estimate=pl.CostEstimate(flops=8_000_000_000, bytes_accessed=8_000_000, transcendentals=0),
        name="forward",
    )(counts, block_rows, offsets, before, source, after, quad, flat_weight, flat_cot)
    inner, west, east = pl.pallas_call(
        backward_kernel,
        out_shape=[
            jax.ShapeDtypeStruct((lat, cols, ch), jnp.float32),
            jax.ShapeDtypeStruct((lat, reach, ch), jnp.bfloat16),
            jax.ShapeDtypeStruct((lat, reach, ch), jnp.bfloat16),
        ],
        in_specs=[SM] * 3 + [VM] * 3,
        out_specs=[VM] * 3,
        scratch_shapes=[
            pltpu.VMEM((lat, wide, ch), jnp.float32),
            pltpu.VMEM((filters * cols, blocks * 128), jnp.bfloat16),
            pltpu.VMEM((lat, filters * cols, ch), jnp.bfloat16),
        ],
        compiler_params=params,
        cost_estimate=pl.CostEstimate(flops=8_000_000_000, bytes_accessed=8_000_000, transcendentals=0),
        name="backward",
    )(counts, block_rows, offsets, quad, flat_weight, flat_cot)
    groups = peers // 4
    summed = pl.pallas_call(
        sum_kernel,
        out_shape=jax.ShapeDtypeStruct((2, 2, groups, chunk, ch), jnp.bfloat16),
        in_specs=[VM],
        out_specs=VM,
        scratch_shapes=[pltpu.VMEM((2, groups, chunk, ch), jnp.bfloat16)]
        + [pltpu.VMEM((groups, chunk, ch), jnp.bfloat16)] * 4
        + [pltpu.SemaphoreType.DMA((6, 2, 2 * groups))],
        compiler_params=pltpu.CompilerParams(
            vmem_limit_bytes=32 * 2**20, collective_id=0, has_side_effects=True
        ),
        cost_estimate=pl.CostEstimate(flops=30_000_000_000, bytes_accessed=60_000_000, transcendentals=0),
        name="weight_sum",
    )(local.reshape(2, 2, groups, chunk, ch))
    summed = summed.reshape(peers * chunk, ch)[: filters * ch].astype(jnp.float32)
    factor = 1.0 / math.sqrt(lat * cols * peers)
    grad_weight = (summed * factor).reshape(filters, ch, ch)
    west_in = lax.ppermute(east, "lon", up).astype(jnp.float32)
    east_in = lax.ppermute(west, "lon", down).astype(jnp.float32)
    inner = inner.at[:, :reach].add(west_in)
    grad_source = inner.at[:, cols - reach :].add(east_in)
    return (mixed.reshape(lat, cols, ch), grad_source, grad_weight)


def solution(mesh):
    return jax.shard_map(
        shards,
        mesh=mesh,
        in_specs=(P("groups", "lon", None), P(), P(), P(), P(), P(), P("groups", "lon", None)),
        out_specs=(P("groups", "lon", None), P("groups", "lon", None), P("groups", None, None)),
        check_vma=False,
    )
```

```python
import math

import jax
import jax.numpy as jnp
from jax import lax
from jax.experimental import pallas as pl
from jax.experimental.pallas import tpu as pltpu
from jax.sharding import PartitionSpec as P

VM = pl.BlockSpec(memory_space=pltpu.VMEM)
MESH = pl.DeviceIdType.MESH
SM = pl.BlockSpec(memory_space=pltpu.SMEM)


def by_count(count, blocks, run):
    for n in range(2, blocks + 1, 2):
        pl.when((count > n - 2) & (count <= n))(lambda n=n: run(n))


def build_band(i, counts, quad, band, filters, blocks, cols):
    for b in range(blocks):
        live = (b < counts[i]).astype(jnp.float32)
        for k in range(filters):
            row = quad[k, i, pl.ds(b, 1), :] * live
            wide = jnp.broadcast_to(row, (cols, row.shape[1]))
            wide = pltpu.roll(wide, 0, 1, stride=1, stride_axis=0)
            band[k * cols : (k + 1) * cols, b * 128 : (b + 1) * 128] = wide.astype(jnp.bfloat16)


def forward_kernel(counts, rows, offs, before, source, after, quad, basis, ext, band, picked):
    lat, cols, ch = source.shape
    filters = quad.shape[0]
    blocks = rows.shape[1]
    reach = before.shape[1]
    ext[:, :reach, :] = before[...].astype(jnp.float32)
    ext[:, reach : reach + cols, :] = source[...].astype(jnp.float32)
    ext[:, reach + cols : 2 * reach + cols, :] = after[...].astype(jnp.float32)

    def live_step(i, blocks):
        build_band(i, counts, quad, band, filters, blocks, cols)
        for b in range(blocks):
            start = offs[i, b] + reach
            shift = start % 8
            near = ext[rows[i, b], pl.ds(pl.multiple_of(start - shift, 8), 136), :].reshape(17, 8, ch)
            near = pltpu.roll(near, (8 - shift) % 8, 1)
            place = lax.broadcasted_iota(jnp.int32, (16, 8, ch), 1)
            near = jnp.where(place < 8 - shift, near[:16], near[1:]).reshape(128, ch)
            picked[b * 128 : (b + 1) * 128, :] = near.astype(jnp.bfloat16)
        here = pl.ds(pl.multiple_of(i * cols, cols), cols)
        used = slice(0, blocks * 128)
        out = jnp.dot(band[:, used], picked[used, :], preferred_element_type=jnp.float32).astype(jnp.bfloat16)
        for k in range(filters):
            basis[here, k * ch : (k + 1) * ch] = out[k * cols : (k + 1) * cols]

    def step(i, _):
        by_count(counts[i], blocks, lambda n: live_step(i, n))
        return 0

    lax.fori_loop(0, lat, step, 0)
    spare = basis.shape[1] - filters * ch
    if spare > 0:
        basis[:, filters * ch :] = jnp.zeros((lat * cols, spare), jnp.bfloat16)


def backward_kernel(counts, rows, offs, quad, weight, cot, inner, west, east, total, band, grads):
    lat, cols, ch = inner.shape
    filters = quad.shape[0]
    blocks = rows.shape[1]
    reach = west.shape[1]
    total[...] = jnp.zeros_like(total)
    for k in range(filters):
        part = lax.dot_general(
            cot[...],
            weight[k * ch : (k + 1) * ch, :],
            (((1,), (1,)), ((), ())),
            preferred_element_type=jnp.float32,
        ).astype(jnp.bfloat16)
        grads[:, k * cols : (k + 1) * cols, :] = part.reshape(lat, cols, ch)

    def live_step(i, blocks):
        build_band(i, counts, quad, band, filters, blocks, cols)
        parts = lax.dot_general(
            band[:, : blocks * 128], grads[i], (((0,), (0,)), ((), ())), preferred_element_type=jnp.float32
        )
        for b in range(blocks):
            start = offs[i, b] + reach
            shift = start % 8
            far = pltpu.roll(parts[b * 128 : (b + 1) * 128].reshape(16, 8, ch), shift, 1)
            zero = jnp.zeros((1, 8, ch), jnp.float32)
            place = lax.broadcasted_iota(jnp.int32, (17, 8, ch), 1)
            far = jnp.where(
                place >= shift, jnp.concatenate([far, zero], axis=0), jnp.concatenate([zero, far], axis=0)
            )
            here = pl.ds(pl.multiple_of(start - shift, 8), 136)
            total[rows[i, b], here, :] += far.reshape(136, ch)

    def step(i, _):
        by_count(counts[i], blocks, lambda n: live_step(i, n))
        return 0

    lax.fori_loop(0, lat, step, 0)
    west[...] = total[:, :reach, :].astype(jnp.bfloat16)
    inner[...] = total[:, reach : reach + cols, :]
    east[...] = total[:, reach + cols : 2 * reach + cols, :].astype(jnp.bfloat16)


def sum_kernel(basis, weight, cot, mixed, out, mine, paired, half, level, partial, others, sems):
    groups, rows, ch = partial.shape
    me = lax.axis_index("lon")
    core = lax.rem(me, 2)
    side = lax.rem(lax.div(me, 2), 2)
    ring = lax.div(me, 4)
    sibling = me + 1 - 2 * core
    across = me + 2 - 4 * side
    spot = [lax.rem(ring + d, groups) for d in range(groups)]
    peer = [spot[d] * 4 + side * 2 + core for d in range(groups)]
    barrier = pltpu.get_barrier_semaphore()
    for other in [sibling, across] + peer[1:]:
        pl.semaphore_signal(barrier, inc=1, device_id={"lon": other}, device_id_type=MESH)
    pl.semaphore_wait(barrier, groups + 1)

    def send(src, dst, phase, slot, other):
        copy = pltpu.make_async_remote_copy(
            src_ref=src,
            dst_ref=dst,
            send_sem=sems.at[phase, 0, slot],
            recv_sem=sems.at[phase, 1, slot],
            device_id={"lon": other},
            device_id_type=MESH,
        )
        copy.start()
        return copy

    def term(half):
        width = 2 * groups * rows
        here = pl.ds(pl.multiple_of(half * width, 128), width)
        part = lax.dot_general(
            basis[:, here], cot[...], (((0,), (0,)), ((), ())), preferred_element_type=jnp.float32
        )
        mine[half] = part.astype(jnp.bfloat16).reshape(2, groups, rows, ch)

    term(1 - core)
    order = list(range(1, groups)) + [0]
    line = [side, 1 - side]
    pairs = {}
    for t in (1, 0):
        for d in order:
            pairs[t, d] = send(mine.at[1 - core, line[t], spot[d]], paired.at[t, d], 0, t * groups + d, sibling)

    term(core)

    def both(t, d):
        pairs[t, d].wait()
        return mine[core, line[t], spot[d]].astype(jnp.float32) + paired[t, d].astype(jnp.float32)

    sides = {}
    for d in order:
        half[d] = both(1, d).astype(jnp.bfloat16)
        sides[d] = send(half.at[d], level.at[d], 1, d, across)
    crossing = {}
    for d in order:
        own = both(0, d)
        sides[d].wait()
        own = own + level[d].astype(jnp.float32)
        if d > 0:
            partial[d] = own.astype(jnp.bfloat16)
            crossing[d] = send(partial.at[d], others.at[d], 2, d, peer[d])
    tile = 256

    def mix(m, _):
        here = pl.ds(pl.multiple_of(m * tile, tile), tile)
        known = basis[here, : weight.shape[0]]
        mixed[here, :] = jnp.dot(known, weight[...], preferred_element_type=jnp.float32).astype(jnp.bfloat16)
        return 0

    lax.fori_loop(0, mixed.shape[0] // tile, mix, 0)
    for d in range(1, groups):
        crossing[d].wait()
        own = own + others[d].astype(jnp.float32)
    out[core, side, ring] = own.astype(jnp.bfloat16)

    def share(c, slot, phase, place, other):
        ref = out.at[core, c, place]
        return send(ref, ref, phase, slot, other)

    far = [share(side, d, 3, ring, peer[d]) for d in range(1, groups)]
    near = []
    last = []
    for d in range(groups):
        if d > 0:
            far[d - 1].wait()
        came = lax.rem(ring - d + groups, groups)
        near.append(share(side, d, 4, came, across))
        last.append(share(side, d, 5, came, sibling))
    for d in range(groups):
        near[d].wait()
        came = lax.rem(ring - d + groups, groups)
        last.append(share(1 - side, groups + d, 5, came, sibling))
    for one in last:
        one.wait()


def shards(source, quadrature, block_rows, offsets, counts, weight, cotangent):
    lat, cols, ch = source.shape
    filters = weight.shape[0]
    blocks = block_rows.shape[1]
    reach = quadrature.shape[3]
    peers = lax.axis_size("lon")
    up = [(i, (i + 1) % peers) for i in range(peers)]
    down = [(j, i) for i, j in up]
    before = lax.ppermute(source[:, cols - reach :], "lon", up)
    after = lax.ppermute(source[:, :reach], "lon", down)
    quad = jnp.pad(quadrature.astype(jnp.float32), ((0, 0), (0, 0), (0, 0), (0, 128 - reach)))
    flat_weight = weight.reshape(filters * ch, ch)
    flat_cot = cotangent.reshape(lat * cols, ch)
    params = pltpu.CompilerParams(vmem_limit_bytes=48 * 2**20)
    chunk = -(-filters * ch // (16 * peers)) * 16
    wide = cols + 2 * reach + 8
    basis = pl.pallas_call(
        forward_kernel,
        out_shape=jax.ShapeDtypeStruct((lat * cols, peers * chunk), jnp.bfloat16),
        in_specs=[SM] * 3 + [VM] * 4,
        out_specs=VM,
        scratch_shapes=[
            pltpu.VMEM((lat, wide, ch), jnp.float32),
            pltpu.VMEM((filters * cols, blocks * 128), jnp.bfloat16),
            pltpu.VMEM((blocks * 128, ch), jnp.bfloat16),
        ],
        compiler_params=pltpu.CompilerParams(vmem_limit_bytes=32 * 2**20),
        cost_estimate=pl.CostEstimate(flops=8_000_000_000, bytes_accessed=8_000_000, transcendentals=0),
        name="forward",
    )(counts, block_rows, offsets, before, source, after, quad)
    inner, west, east = pl.pallas_call(
        backward_kernel,
        out_shape=[
            jax.ShapeDtypeStruct((lat, cols, ch), jnp.float32),
            jax.ShapeDtypeStruct((lat, reach, ch), jnp.bfloat16),
            jax.ShapeDtypeStruct((lat, reach, ch), jnp.bfloat16),
        ],
        in_specs=[SM] * 3 + [VM] * 3,
        out_specs=[VM] * 3,
        scratch_shapes=[
            pltpu.VMEM((lat, wide, ch), jnp.float32),
            pltpu.VMEM((filters * cols, blocks * 128), jnp.bfloat16),
            pltpu.VMEM((lat, filters * cols, ch), jnp.bfloat16),
        ],
        compiler_params=params,
        cost_estimate=pl.CostEstimate(flops=8_000_000_000, bytes_accessed=8_000_000, transcendentals=0),
        name="backward",
    )(counts, block_rows, offsets, quad, flat_weight, flat_cot)
    groups = peers // 4
    mixed, summed = pl.pallas_call(
        sum_kernel,
        out_shape=[
            jax.ShapeDtypeStruct((lat * cols, ch), jnp.bfloat16),
            jax.ShapeDtypeStruct((2, 2, groups, chunk, ch), jnp.bfloat16),
        ],
        in_specs=[VM] * 3,
        out_specs=[VM] * 2,
        scratch_shapes=[pltpu.VMEM((2, 2, groups, chunk, ch), jnp.bfloat16)]
        + [pltpu.VMEM((2, groups, chunk, ch), jnp.bfloat16)]
        + [pltpu.VMEM((groups, chunk, ch), jnp.bfloat16)] * 4
        + [pltpu.SemaphoreType.DMA((6, 2, 2 * groups))],
        compiler_params=pltpu.CompilerParams(
            vmem_limit_bytes=32 * 2**20, collective_id=0, has_side_effects=True
        ),
        cost_estimate=pl.CostEstimate(flops=30_000_000_000, bytes_accessed=60_000_000, transcendentals=0),
        name="weight_sum",
    )(basis, flat_weight, flat_cot)
    summed = summed.reshape(peers * chunk, ch)[: filters * ch].astype(jnp.float32)
    factor = 1.0 / math.sqrt(lat * cols * peers)
    grad_weight = (summed * factor).reshape(filters, ch, ch)
    west_in = lax.ppermute(east, "lon", up).astype(jnp.float32)
    east_in = lax.ppermute(west, "lon", down).astype(jnp.float32)
    inner = inner.at[:, :reach].add(west_in)
    grad_source = inner.at[:, cols - reach :].add(east_in)
    return (mixed.reshape(lat, cols, ch), grad_source, grad_weight)


def solution(mesh):
    return jax.shard_map(
        shards,
        mesh=mesh,
        in_specs=(P("groups", "lon", None), P(), P(), P(), P(), P(), P("groups", "lon", None)),
        out_specs=(P("groups", "lon", None), P("groups", "lon", None), P("groups", None, None)),
        check_vma=False,
    )
```

```python
import math

import jax
import jax.numpy as jnp
from jax import lax
from jax.experimental import pallas as pl
from jax.experimental.pallas import tpu as pltpu
from jax.sharding import PartitionSpec as P

VM = pl.BlockSpec(memory_space=pltpu.VMEM)
MESH = pl.DeviceIdType.MESH
SM = pl.BlockSpec(memory_space=pltpu.SMEM)


def by_count(count, blocks, run):
    for n in range(2, blocks + 1, 2):
        pl.when((count > n - 2) & (count <= n))(lambda n=n: run(n))


def build_band(i, counts, quad, band, filters, blocks, cols):
    for b in range(blocks):
        live = (b < counts[i]).astype(jnp.float32)
        for k in range(filters):
            row = quad[k, b, pl.ds(i, 1), :] * live
            wide = jnp.broadcast_to(row, (cols, row.shape[1]))
            wide = pltpu.roll(wide, 0, 1, stride=1, stride_axis=0)
            band[k * cols : (k + 1) * cols, b * 128 : (b + 1) * 128] = wide.astype(jnp.bfloat16)


def forward_kernel(counts, rows, offs, before, source, after, quad, basis, ext, band, picked):
    lat, cols, ch = source.shape
    filters = quad.shape[0]
    blocks = rows.shape[0]
    reach = before.shape[1]
    ext[:, :reach, :] = before[...].astype(jnp.float32)
    ext[:, reach : reach + cols, :] = source[...].astype(jnp.float32)
    ext[:, reach + cols : 2 * reach + cols, :] = after[...].astype(jnp.float32)

    def live_step(i, blocks):
        build_band(i, counts, quad, band, filters, blocks, cols)
        for b in range(blocks):
            start = offs[b, i] + reach
            shift = start % 8
            near = ext[rows[b, i], pl.ds(pl.multiple_of(start - shift, 8), 136), :].reshape(17, 8, ch)
            near = pltpu.roll(near, (8 - shift) % 8, 1)
            place = lax.broadcasted_iota(jnp.int32, (16, 8, ch), 1)
            near = jnp.where(place < 8 - shift, near[:16], near[1:]).reshape(128, ch)
            picked[b * 128 : (b + 1) * 128, :] = near.astype(jnp.bfloat16)
        here = pl.ds(pl.multiple_of(i * cols, cols), cols)
        used = slice(0, blocks * 128)
        out = jnp.dot(band[:, used], picked[used, :], preferred_element_type=jnp.float32).astype(jnp.bfloat16)
        for k in range(filters):
            basis[here, k * ch : (k + 1) * ch] = out[k * cols : (k + 1) * cols]

    def step(i, _):
        by_count(counts[i], blocks, lambda n: live_step(i, n))
        return 0

    lax.fori_loop(0, lat, step, 0)
    spare = basis.shape[1] - filters * ch
    if spare > 0:
        basis[:, filters * ch :] = jnp.zeros((lat * cols, spare), jnp.bfloat16)


def backward_kernel(counts, rows, offs, quad, weight, cot, inner, west, east, total, band, grads):
    lat, cols, ch = inner.shape
    filters = quad.shape[0]
    blocks = rows.shape[0]
    reach = west.shape[1]
    total[...] = jnp.zeros_like(total)
    for k in range(filters):
        part = lax.dot_general(
            cot[...],
            weight[k * ch : (k + 1) * ch, :],
            (((1,), (1,)), ((), ())),
            preferred_element_type=jnp.float32,
        ).astype(jnp.bfloat16)
        grads[:, k * cols : (k + 1) * cols, :] = part.reshape(lat, cols, ch)

    def live_step(i, blocks):
        build_band(i, counts, quad, band, filters, blocks, cols)
        parts = lax.dot_general(
            band[:, : blocks * 128], grads[i], (((0,), (0,)), ((), ())), preferred_element_type=jnp.float32
        )
        for b in range(blocks):
            start = offs[b, i] + reach
            shift = start % 8
            far = pltpu.roll(parts[b * 128 : (b + 1) * 128].reshape(16, 8, ch), shift, 1)
            zero = jnp.zeros((1, 8, ch), jnp.float32)
            place = lax.broadcasted_iota(jnp.int32, (17, 8, ch), 1)
            far = jnp.where(
                place >= shift, jnp.concatenate([far, zero], axis=0), jnp.concatenate([zero, far], axis=0)
            )
            here = pl.ds(pl.multiple_of(start - shift, 8), 136)
            total[rows[b, i], here, :] += far.reshape(136, ch)

    def step(i, _):
        by_count(counts[i], blocks, lambda n: live_step(i, n))
        return 0

    lax.fori_loop(0, lat, step, 0)
    west[...] = total[:, :reach, :].astype(jnp.bfloat16)
    inner[...] = total[:, reach : reach + cols, :]
    east[...] = total[:, reach + cols : 2 * reach + cols, :].astype(jnp.bfloat16)


def sum_kernel(basis, weight, cot, mixed, out, mine, paired, half, level, partial, others, sems):
    groups, rows, ch = partial.shape
    me = lax.axis_index("lon")
    core = lax.rem(me, 2)
    side = lax.rem(lax.div(me, 2), 2)
    ring = lax.div(me, 4)
    sibling = me + 1 - 2 * core
    across = me + 2 - 4 * side
    spot = [lax.rem(ring + d, groups) for d in range(groups)]
    peer = [spot[d] * 4 + side * 2 + core for d in range(groups)]
    barrier = pltpu.get_barrier_semaphore()
    for other in [sibling, across] + peer[1:]:
        pl.semaphore_signal(barrier, inc=1, device_id={"lon": other}, device_id_type=MESH)
    pl.semaphore_wait(barrier, groups + 1)

    def send(src, dst, phase, slot, other):
        copy = pltpu.make_async_remote_copy(
            src_ref=src,
            dst_ref=dst,
            send_sem=sems.at[phase, 0, slot],
            recv_sem=sems.at[phase, 1, slot],
            device_id={"lon": other},
            device_id_type=MESH,
        )
        copy.start()
        return copy

    def term(half):
        width = 2 * groups * rows
        here = pl.ds(pl.multiple_of(half * width, 128), width)
        part = lax.dot_general(
            basis[:, here], cot[...], (((0,), (0,)), ((), ())), preferred_element_type=jnp.float32
        )
        mine[half] = part.astype(jnp.bfloat16).reshape(2, groups, rows, ch)

    term(1 - core)
    order = list(range(1, groups)) + [0]
    line = [side, 1 - side]
    pairs = {}
    for t in (1, 0):
        for d in order:
            pairs[t, d] = send(mine.at[1 - core, line[t], spot[d]], paired.at[t, d], 0, t * groups + d, sibling)

    term(core)

    def both(t, d):
        pairs[t, d].wait()
        return mine[core, line[t], spot[d]].astype(jnp.float32) + paired[t, d].astype(jnp.float32)

    sides = {}
    for d in order:
        half[d] = both(1, d).astype(jnp.bfloat16)
        sides[d] = send(half.at[d], level.at[d], 1, d, across)
    crossing = {}
    for d in order:
        own = both(0, d)
        sides[d].wait()
        own = own + level[d].astype(jnp.float32)
        if d > 0:
            partial[d] = own.astype(jnp.bfloat16)
            crossing[d] = send(partial.at[d], others.at[d], 2, d, peer[d])
    tile = 256

    def mix(m, _):
        here = pl.ds(pl.multiple_of(m * tile, tile), tile)
        known = basis[here, : weight.shape[0]]
        mixed[here, :] = jnp.dot(known, weight[...], preferred_element_type=jnp.float32).astype(jnp.bfloat16)
        return 0

    lax.fori_loop(0, mixed.shape[0] // tile, mix, 0)
    for d in range(1, groups):
        crossing[d].wait()
        own = own + others[d].astype(jnp.float32)
    out[core, side, ring] = own.astype(jnp.bfloat16)

    def share(c, slot, phase, place, other):
        ref = out.at[core, c, place]
        return send(ref, ref, phase, slot, other)

    far = [share(side, d, 3, ring, peer[d]) for d in range(1, groups)]
    near = []
    last = []
    for d in range(groups):
        if d > 0:
            far[d - 1].wait()
        came = lax.rem(ring - d + groups, groups)
        near.append(share(side, d, 4, came, across))
        last.append(share(side, d, 5, came, sibling))
    for d in range(groups):
        near[d].wait()
        came = lax.rem(ring - d + groups, groups)
        last.append(share(1 - side, groups + d, 5, came, sibling))
    for one in last:
        one.wait()


def shards(source, quadrature, block_rows, offsets, counts, weight, cotangent):
    lat, cols, ch = source.shape
    filters = weight.shape[0]
    blocks = block_rows.shape[1]
    reach = quadrature.shape[3]
    peers = lax.axis_size("lon")
    up = [(i, (i + 1) % peers) for i in range(peers)]
    down = [(j, i) for i, j in up]
    before = lax.ppermute(source[:, cols - reach :], "lon", up)
    after = lax.ppermute(source[:, :reach], "lon", down)
    quad = jnp.pad(quadrature.transpose(0, 2, 1, 3).astype(jnp.float32), ((0, 0), (0, 0), (0, 0), (0, 128 - reach)))
    flat_weight = weight.reshape(filters * ch, ch)
    flat_cot = cotangent.reshape(lat * cols, ch)
    params = pltpu.CompilerParams(vmem_limit_bytes=48 * 2**20)
    chunk = -(-filters * ch // (16 * peers)) * 16
    wide = cols + 2 * reach + 8
    basis = pl.pallas_call(
        forward_kernel,
        out_shape=jax.ShapeDtypeStruct((lat * cols, peers * chunk), jnp.bfloat16),
        in_specs=[SM] * 3 + [VM] * 4,
        out_specs=VM,
        scratch_shapes=[
            pltpu.VMEM((lat, wide, ch), jnp.float32),
            pltpu.VMEM((filters * cols, blocks * 128), jnp.bfloat16),
            pltpu.VMEM((blocks * 128, ch), jnp.bfloat16),
        ],
        compiler_params=pltpu.CompilerParams(vmem_limit_bytes=32 * 2**20),
        cost_estimate=pl.CostEstimate(flops=8_000_000_000, bytes_accessed=8_000_000, transcendentals=0),
        name="forward",
    )(counts, block_rows.T, offsets.T, before, source, after, quad)
    inner, west, east = pl.pallas_call(
        backward_kernel,
        out_shape=[
            jax.ShapeDtypeStruct((lat, cols, ch), jnp.float32),
            jax.ShapeDtypeStruct((lat, reach, ch), jnp.bfloat16),
            jax.ShapeDtypeStruct((lat, reach, ch), jnp.bfloat16),
        ],
        in_specs=[SM] * 3 + [VM] * 3,
        out_specs=[VM] * 3,
        scratch_shapes=[
            pltpu.VMEM((lat, wide, ch), jnp.float32),
            pltpu.VMEM((filters * cols, blocks * 128), jnp.bfloat16),
            pltpu.VMEM((lat, filters * cols, ch), jnp.bfloat16),
        ],
        compiler_params=params,
        cost_estimate=pl.CostEstimate(flops=8_000_000_000, bytes_accessed=8_000_000, transcendentals=0),
        name="backward",
    )(counts, block_rows.T, offsets.T, quad, flat_weight, flat_cot)
    groups = peers // 4
    mixed, summed = pl.pallas_call(
        sum_kernel,
        out_shape=[
            jax.ShapeDtypeStruct((lat * cols, ch), jnp.bfloat16),
            jax.ShapeDtypeStruct((2, 2, groups, chunk, ch), jnp.bfloat16),
        ],
        in_specs=[VM] * 3,
        out_specs=[VM] * 2,
        scratch_shapes=[pltpu.VMEM((2, 2, groups, chunk, ch), jnp.bfloat16)]
        + [pltpu.VMEM((2, groups, chunk, ch), jnp.bfloat16)]
        + [pltpu.VMEM((groups, chunk, ch), jnp.bfloat16)] * 4
        + [pltpu.SemaphoreType.DMA((6, 2, 2 * groups))],
        compiler_params=pltpu.CompilerParams(
            vmem_limit_bytes=32 * 2**20, collective_id=0, has_side_effects=True
        ),
        cost_estimate=pl.CostEstimate(flops=30_000_000_000, bytes_accessed=60_000_000, transcendentals=0),
        name="weight_sum",
    )(basis, flat_weight, flat_cot)
    summed = summed.reshape(peers * chunk, ch)[: filters * ch].astype(jnp.float32)
    factor = 1.0 / math.sqrt(lat * cols * peers)
    grad_weight = (summed * factor).reshape(filters, ch, ch)
    west_in = lax.ppermute(east, "lon", up).astype(jnp.float32)
    east_in = lax.ppermute(west, "lon", down).astype(jnp.float32)
    inner = inner.at[:, :reach].add(west_in)
    grad_source = inner.at[:, cols - reach :].add(east_in)
    return (mixed.reshape(lat, cols, ch), grad_source, grad_weight)


def solution(mesh):
    return jax.shard_map(
        shards,
        mesh=mesh,
        in_specs=(P("groups", "lon", None), P(), P(), P(), P(), P(), P("groups", "lon", None)),
        out_specs=(P("groups", "lon", None), P("groups", "lon", None), P("groups", None, None)),
        check_vma=False,
    )
```
